32 devices in a mesh: groups: 2 (over x), blk: 16 (over z, y, core).
Axes of the slice: x: 2, y: 2, z: 4, core: 2. Of those that a mesh axis runs over, the one named last changes fastest.
Arguments:
- hidden: bfloat16 [12288, 5120], P(('groups', 'blk')), parts along dimension 0, may hold values from -6 to 6
- norm_gain: float32 [5120], replicated, may hold values from 0.5 to 1.5
- q_weight: bfloat16 [5120, 2560], P('blk'), may hold values from -0.078125 to 0.078125
- q_bias: float32 [2560], replicated, may hold values from -5 to 5
- kv_store: bfloat16 [128, 2, 512, 512], P(('groups', 'blk')), parts along dimension 0, may hold values from -620 to 620
- block_home: int32 [128], P('groups'), parts along dimension 0, may hold values from 0 to 63, as said below
- need_ids: int32 [64, 2], P(('groups', 'blk')), parts along dimension 0, may hold values from 0 to 63, as said below
- hole_pos: int32 [64], P(('groups', 'blk')), parts along dimension 0, may hold values from 0 to 32767, as said below
- fill_len: int32 [64], P(('groups', 'blk')), parts along dimension 0, may hold values from 48 to 192
Outputs:
- attended: bfloat16 [12288, 2560], P(('groups', 'blk')), parts along dimension 0
The draws below stay inside these ranges and needn't reach their ends.
There are 2 independent parts, one for each index of `groups`. The reference program is written for one: setup_inputs(seed, part) draws one part's arguments, and reference() takes and returns one part's arrays. A program takes and returns all parts, laid end to end along the dimension named above; an argument that names none is the same for every part. Nothing has to cross between parts.
Inputs may be any that keep to these rules, and one draw needn't show every extreme that they name: block_home is a permutation; block b is kept by device block_home[b] // 4 of blk. `need_ids`: the 4 blocks listed by the candidates of one device of blk are all different and are kept by different devices, each at most 2 places away from it along blk, counted around the loop. The span from hole_pos to hole_pos + fill_len - 1 lies inside the first block that the candidate lists.
All inputs are finite; a program needn't handle non-finite values.
Results may differ from the reference program's by a relative error of at most 0.0035.
The reference program's roundings to bfloat16 on the way (of `normed`, `query`, `keys` and `weights`) count: a program that leaves them out, or rounds other values in their place, can miss the bound.
Values may be sent and summed in bfloat16 or wider, within the bound.
A program may use at most 128 MiB of HBM per device.

```python
import math
import jax
import jax.numpy as jnp
from jax import lax

D = 5120
HEAD_SIZE = 128
QUERY_HEADS = 20
KEY_HEADS = 4
BLOCK_TOKENS = 512
BLOCKS_NEEDED = 2
CAND_DEV = 2
REACH = 2
CANDIDATE_ROWS = 192
BLK_DEV = 4
QUERY_PER_KEY = 5
BLOCK_TOTAL = 64
CANDS = 32
ROWS = 6144


def layout_draw(key):
    key_home = jax.random.fold_in(key, 11)
    key_offset = jax.random.fold_in(key, 12)
    key_slot = jax.random.fold_in(key, 13)
    key_fill = jax.random.fold_in(key, 14)
    key_hole = jax.random.fold_in(key, 15)
    device_count = BLOCK_TOTAL // BLK_DEV
    span_size = 2 * REACH + 1
    pick_count = CAND_DEV * BLOCKS_NEEDED
    home_table = jax.random.permutation(key_home, BLOCK_TOTAL).astype(jnp.int32)
    inverse = jnp.argsort(home_table).astype(jnp.int32)
    device_keys = jax.random.split(key_offset, device_count)
    offset_draw = jax.vmap(lambda one_key: jax.random.permutation(one_key, span_size)[:pick_count])(device_keys)
    offset_draw = offset_draw.astype(jnp.int32) - REACH
    slot_draw = jax.random.randint(key_slot, (device_count, pick_count), 0, BLK_DEV).astype(jnp.int32)
    device_ids = jnp.arange(device_count, dtype=jnp.int32)[:, None]
    owners = jnp.remainder(device_ids - offset_draw, device_count)
    stored_at = owners * BLK_DEV + slot_draw
    block_ids = inverse[stored_at.reshape(-1)].reshape(CANDS, BLOCKS_NEEDED)
    fill_draw = jax.random.randint(key_fill, (CANDS,), CANDIDATE_ROWS // 4, CANDIDATE_ROWS + 1).astype(jnp.int32)
    fill_draw = fill_draw.at[0].set(CANDIDATE_ROWS)
    hole_draw = jax.random.randint(key_hole, (CANDS,), 0, BLOCK_TOKENS - fill_draw + 1).astype(jnp.int32)
    hole_draw = block_ids[:, 0] * BLOCK_TOKENS + hole_draw
    return (home_table, block_ids.astype(jnp.int32), hole_draw.astype(jnp.int32), fill_draw)


def draw_block_home(key, part):
    return layout_draw(key)[0]


def draw_need_ids(key, part):
    return layout_draw(key)[1]


def draw_hole_pos(key, part):
    return layout_draw(key)[2]


def draw_fill_len(key, part):
    return layout_draw(key)[3]


def draw_kv_store(key, part):
    base_sample = jnp.clip(jax.random.normal(jax.random.fold_in(key, 31), (BLOCK_TOTAL, 2, BLOCK_TOKENS, KEY_HEADS * HEAD_SIZE), jnp.float32), -6.0, 6.0)
    return base_sample.astype(jnp.bfloat16)


def block_scale(own_key, dims, cuts, low, high):
    level = 1.0
    for dim, blocks in cuts:
        heights = jax.random.uniform(jax.random.fold_in(jax.random.fold_in(own_key, 6), dim), (blocks,), jnp.float32, low / len(cuts), high / len(cuts))
        level = level * jnp.repeat(jnp.exp(heights), dims[dim] // blocks).reshape((-1,) + (1,) * (len(dims) - 1 - dim))
    return level


def gaussian(own_key, shape, scale, most, cuts=(), kind=jnp.bfloat16):
    drawn = scale * jax.random.normal(own_key, shape, jnp.float32)
    if cuts:
        drawn = drawn * block_scale(own_key, shape, cuts, -0.22, 0.18)
    return jnp.clip(drawn, -most, most).astype(kind)


def setup_inputs(seed: int = 0, part: int = 0) -> dict:
    keys = jax.random.split(jax.random.key(seed), 10)
    part_splits = jax.random.split(jax.random.fold_in(keys[9], part), 10)
    hidden = gaussian(part_splits[0], (ROWS, D), 1.0, 6.0, ((0, 16),))
    norm_gain = jnp.clip(1.0 + 0.1 * jax.random.normal(keys[1], (D,), jnp.float32), 0.5, 1.5)
    q_weight = gaussian(keys[2], (D, QUERY_HEADS * HEAD_SIZE), D ** -0.5, 0.078125, ((0, 16),))
    q_bias = gaussian(keys[3], (QUERY_HEADS * HEAD_SIZE,), 1.0, 5.0, (), jnp.float32)
    kv_store = draw_kv_store(jax.random.fold_in(jax.random.fold_in(keys[9], part), 71), part)
    block_home = draw_block_home(jax.random.fold_in(jax.random.fold_in(keys[9], part), 71), part)
    need_ids = draw_need_ids(jax.random.fold_in(jax.random.fold_in(keys[9], part), 71), part)
    hole_pos = draw_hole_pos(jax.random.fold_in(jax.random.fold_in(keys[9], part), 71), part)
    fill_len = draw_fill_len(jax.random.fold_in(jax.random.fold_in(keys[9], part), 71), part)
    return dict(hidden=hidden, norm_gain=norm_gain, q_weight=q_weight, q_bias=q_bias, kv_store=kv_store, block_home=block_home, need_ids=need_ids, hole_pos=hole_pos, fill_len=fill_len)


def rms_normed(hidden, norm_gain):
    widened = hidden.astype(jnp.float32)
    scale_inv = lax.rsqrt(lax.optimization_barrier(jnp.mean(widened * widened, axis=-1, keepdims=True)) + 1e-06)
    return (widened * scale_inv * norm_gain).astype(jnp.bfloat16)

def attend_one(candidate_query_rows, sketch_blocks, block_ids, hole_start, fill_rows):
    block_key_rows = sketch_blocks[:, 0].reshape(BLOCKS_NEEDED * BLOCK_TOKENS, KEY_HEADS, HEAD_SIZE).astype(jnp.float32)
    block_value_rows = sketch_blocks[:, 1].reshape(BLOCKS_NEEDED * BLOCK_TOKENS, KEY_HEADS, HEAD_SIZE).astype(jnp.float32)
    query_matrix = candidate_query_rows.reshape(CANDIDATE_ROWS, KEY_HEADS, QUERY_PER_KEY, HEAD_SIZE).astype(jnp.float32)
    scores = jnp.einsum('rkgd,tkd->rkgt', query_matrix, block_key_rows) / math.sqrt(HEAD_SIZE)
    position = (block_ids[:, None] * BLOCK_TOKENS + jnp.arange(BLOCK_TOKENS, dtype=jnp.int32)[None, :]).reshape(-1)
    masked = (position >= hole_start) & (position < hole_start + fill_rows)
    scores = jnp.where(masked[None, None, None, :], jnp.float32(-1e+30), scores)
    row_max = lax.optimization_barrier(jnp.max(scores, axis=-1, keepdims=True))
    exponent = jnp.exp(scores - row_max)
    denominator = lax.optimization_barrier(jnp.sum(exponent, axis=-1))
    weights = exponent.astype(jnp.bfloat16)
    attended = jnp.einsum('rkgt,tkd->rkgd', weights.astype(jnp.float32), block_value_rows) / denominator[..., None]
    attended = attended.reshape(CANDIDATE_ROWS, QUERY_HEADS * HEAD_SIZE)
    live_rows = jnp.arange(CANDIDATE_ROWS, dtype=jnp.int32) < fill_rows
    return jnp.where(live_rows[:, None], attended, jnp.float32(0.0)).astype(jnp.bfloat16)

def reference(hidden, norm_gain, q_weight, q_bias, kv_store, block_home, need_ids, hole_pos, fill_len):
    normed = rms_normed(hidden, norm_gain)
    query = (jnp.dot(normed, q_weight, preferred_element_type=jnp.float32) + q_bias).astype(jnp.bfloat16)
    stored_at = block_home[need_ids]

    def one_candidate(packed):
        candidate_query_rows, stored_rows, block_ids, hole_start, fill_rows = packed
        sketch_blocks = kv_store[stored_rows]
        return attend_one(candidate_query_rows, sketch_blocks, block_ids, hole_start, fill_rows)
    results = lax.map(one_candidate, (query.reshape(CANDS, CANDIDATE_ROWS, QUERY_HEADS * HEAD_SIZE), stored_at, need_ids, hole_pos, fill_len))
    return results.reshape(ROWS, QUERY_HEADS * HEAD_SIZE)
```

```python
import math

import jax
import jax.numpy as jnp
from jax import lax
from jax.experimental import pallas as pl
from jax.experimental.pallas import tpu as pltpu
from jax.sharding import PartitionSpec as P

HEAD_SIZE = 128
QUERY_HEADS = 20
KEY_HEADS = 4
BLOCK_TOKENS = 512
BLOCKS_NEEDED = 2
REACH = 2


def passed_along(block, axis, distance):
    devices = range(lax.axis_size(axis))
    route = [((i - distance) % len(devices), i) for i in devices]
    return lax.ppermute(block, axis, route)


def rms_normed(hidden, norm_gain):
    widened = hidden.astype(jnp.float32)
    scale_inv = lax.rsqrt(jnp.mean(widened * widened, axis=-1, keepdims=True) + 1e-06)
    return (widened * scale_inv * norm_gain).astype(jnp.bfloat16)


def attend_kernel(slots, hole, fill, q_ref, first_ref, second_ref, out_ref):
    cand = pl.program_id(0)
    rows = q_ref.shape[0]
    factor = math.log2(math.e) / math.sqrt(HEAD_SIZE)
    live = fill[cand]
    start = hole[cand]
    column = lax.broadcasted_iota(jnp.int32, (rows, BLOCK_TOKENS), 1)
    masked = (column >= start) & (column < start + live)
    alive = lax.broadcasted_iota(jnp.int32, (rows, HEAD_SIZE), 0) < live
    over_keys = (((1,), (1,)), ((), ()))
    for head in range(QUERY_HEADS // KEY_HEADS):
        place = pl.ds(head * HEAD_SIZE, HEAD_SIZE)
        q = q_ref[:, place]
        near = lax.dot_general(q, first_ref[0, 0], over_keys, preferred_element_type=jnp.float32)
        far = lax.dot_general(q, second_ref[0, 0], over_keys, preferred_element_type=jnp.float32)
        near = jnp.where(masked, jnp.float32(-1e30), near)
        most = jnp.maximum(
            jnp.max(near, axis=-1, keepdims=True), jnp.max(far, axis=-1, keepdims=True)
        )
        near = jnp.exp2((near - most) * factor)
        far = jnp.exp2((far - most) * factor)
        total = jnp.sum(near, axis=-1, keepdims=True) + jnp.sum(far, axis=-1, keepdims=True)
        mixed = jnp.dot(
            near.astype(jnp.bfloat16), first_ref[0, 1], preferred_element_type=jnp.float32
        ) + jnp.dot(
            far.astype(jnp.bfloat16), second_ref[0, 1], preferred_element_type=jnp.float32
        )
        out_ref[:, place] = jnp.where(alive, mixed / total, 0.0).astype(jnp.bfloat16)


def attend(query, arrived, slots, need_ids, hole_pos, fill_len):
    cands = need_ids.shape[0]
    rows = query.shape[0] // cands
    width = QUERY_HEADS // KEY_HEADS * HEAD_SIZE
    hole = hole_pos - need_ids[:, 0] * BLOCK_TOKENS

    def sketch(entry):
        return pl.BlockSpec(
            (1, 2, BLOCK_TOKENS, HEAD_SIZE),
            lambda c, k, slots, hole, fill: (slots[c * BLOCKS_NEEDED + entry], 0, 0, k),
        )

    by_head = pl.BlockSpec((rows, width), lambda c, k, slots, hole, fill: (c, k))
    return pl.pallas_call(
        attend_kernel,
        grid_spec=pltpu.PrefetchScalarGridSpec(
            num_scalar_prefetch=3,
            grid=(cands, KEY_HEADS),
            in_specs=[by_head, sketch(0), sketch(1)],
            out_specs=by_head,
        ),
        out_shape=jax.ShapeDtypeStruct(query.shape, jnp.bfloat16),
        compiler_params=pltpu.CompilerParams(vmem_limit_bytes=40 * 1024 * 1024),
    )(slots.reshape(-1), hole, fill_len, query, arrived, arrived)


def shards(hidden, norm_gain, q_weight, q_bias, kv_store, block_home, need_ids, hole_pos, fill_len):
    normed = rms_normed(hidden, norm_gain)
    whole_weight = lax.all_gather(q_weight, "blk", axis=0, tiled=True)
    projected = jnp.dot(normed, whole_weight, preferred_element_type=jnp.float32)
    query = (projected + q_bias).astype(jnp.bfloat16)
    device_count = lax.axis_size("blk")
    myself = lax.axis_index("blk")
    local_count = kv_store.shape[0]
    empty_block = jnp.zeros(kv_store.shape[1:], kv_store.dtype)

    def select_block(block_lists):
        stored_at = block_home[block_lists.reshape(-1)]
        owned_here = stored_at // local_count == myself
        slot_index = jnp.sum(jnp.where(owned_here, stored_at % local_count, 0))
        has_block = jnp.any(owned_here)
        chosen = lax.dynamic_index_in_dim(kv_store, slot_index, 0, keepdims=False)
        return jnp.where(has_block, chosen, empty_block)

    incoming = []
    for offset in range(-REACH, REACH + 1):
        if offset == 0:
            incoming.append(select_block(need_ids))
        else:
            asked = passed_along(need_ids, "blk", -offset)
            incoming.append(passed_along(select_block(asked), "blk", offset))
    arrived = jnp.stack(incoming, axis=0)
    owners = block_home[need_ids] // local_count
    slot_of_entry = jnp.remainder(myself - owners + REACH, device_count)
    return attend(query, arrived, slot_of_entry, need_ids, hole_pos, fill_len)


def solution(mesh):
    placed = (
        P(("groups", "blk"), None),
        P(),
        P("blk", None),
        P(),
        P(("groups", "blk"), None, None, None),
        P("groups"),
        P(("groups", "blk"), None),
        P(("groups", "blk")),
        P(("groups", "blk")),
    )
    return jax.shard_map(
        shards, mesh=mesh, in_specs=placed, out_specs=P(("groups", "blk"), None), check_vma=False
    )
```

```python
import functools
import math

import jax
import jax.numpy as jnp
from jax import lax
from jax.experimental import pallas as pl
from jax.experimental.pallas import tpu as pltpu
from jax.sharding import PartitionSpec as P

HEAD_SIZE = 128
QUERY_HEADS = 20
KEY_HEADS = 4
BLOCK_TOKENS = 512
BLOCKS_NEEDED = 2
REACH = 2
MESH = pl.DeviceIdType.MESH


def exchange_kernel(ids_ref, out_ref, send_sem, recv_sem):
    count = lax.axis_size("blk")
    me = lax.axis_index("blk")
    barrier = pltpu.get_barrier_semaphore()
    offsets = [o for o in range(-REACH, REACH + 1) if o]
    for o in offsets:
        pl.semaphore_signal(
            barrier, inc=1, device_id={"blk": lax.rem(me + o + count, count)}, device_id_type=MESH
        )
    pl.semaphore_wait(barrier, len(offsets))
    copies = []
    for o in offsets:
        copy = pltpu.make_async_remote_copy(
            src_ref=ids_ref,
            dst_ref=out_ref.at[o + REACH],
            send_sem=send_sem.at[o + REACH],
            recv_sem=recv_sem.at[o + REACH],
            device_id={"blk": lax.rem(me - o + count, count)},
            device_id_type=MESH,
        )
        copy.start()
        copies.append(copy)
    out_ref[REACH] = ids_ref[...]
    for copy in copies:
        copy.wait()


def exchanged(need_ids):
    cands, needed = need_ids.shape
    padded = jnp.pad(need_ids, ((0, 8 - cands), (0, 128 - needed)))
    span = 2 * REACH + 1
    out = pl.pallas_call(
        exchange_kernel,
        out_shape=jax.ShapeDtypeStruct((span, 8, 128), jnp.int32),
        in_specs=[pl.BlockSpec(memory_space=pltpu.VMEM)],
        out_specs=pl.BlockSpec(memory_space=pltpu.VMEM),
        scratch_shapes=[pltpu.SemaphoreType.DMA((span,)), pltpu.SemaphoreType.DMA((span,))],
        compiler_params=pltpu.CompilerParams(collective_id=0, has_side_effects=True),
    )(padded)
    return out[:, :cands, :needed].reshape(span, cands * needed)


def pick_kernel(slots, in_ref, out_ref):
    out_ref[...] = in_ref[...]


def picked_blocks(slots, kv_store):
    block = (1,) + kv_store.shape[1:]
    return pl.pallas_call(
        pick_kernel,
        grid_spec=pltpu.PrefetchScalarGridSpec(
            num_scalar_prefetch=1,
            grid=slots.shape,
            in_specs=[pl.BlockSpec(block, lambda i, slots: (slots[i], 0, 0, 0))],
            out_specs=pl.BlockSpec(block, lambda i, slots: (i, 0, 0, 0)),
        ),
        out_shape=jax.ShapeDtypeStruct(slots.shape + kv_store.shape[1:], kv_store.dtype),
        compiler_params=pltpu.CompilerParams(vmem_limit_bytes=16 * 1024 * 1024),
    )(slots, kv_store)


def project_kernel(
    chips, snake, hidden, gain, weight, bias, picked, query, arrived,
    whole, normed, acc, recv, to_ahead, to_behind, to_sibling, to_partner, kv_send, kv_recv, kv_own,
):
    group, me = lax.axis_index("groups"), lax.axis_index("blk")
    count = 2 * chips
    half = chips // 2
    place, core, side = lax.div(me, 2), lax.rem(me, 2), lax.rem(group, 2)
    depth, width = weight.shape[0], weight.shape[1] // 2

    def ring_of(chip):
        if not snake:
            return chip
        z, y = lax.div(chip, 2), lax.rem(chip, 2)
        return z + y * (chips - 1 - 2 * z)

    def chip_of(spot):
        spot = lax.rem(spot + chips, chips)
        if not snake:
            return spot
        y = lax.div(spot, half)
        return (spot + y * (chips - 1 - 2 * spot)) * 2 + y

    spot = ring_of(place)
    turn = 1 - 2 * core
    ahead = {"blk": chip_of(spot + turn) * 2 + core}
    behind = {"blk": chip_of(spot - turn) * 2 + core}
    sibling = {"blk": me + turn}
    partner = {"groups": group + 1 - 2 * side}
    offsets = [o for o in (1, -1, 2, -2)]

    def near(o):
        return {"blk": lax.rem(me + o + count, count)}

    greeted = [ahead, behind, sibling, partner] + [near(o) for o in offsets]
    barrier = pltpu.get_barrier_semaphore()
    for other in greeted:
        pl.semaphore_signal(barrier, inc=1, device_id=other, device_id_type=MESH)
    for h in range(2):
        whole[place, h, core] = weight[:, h * width : (h + 1) * width]
    pl.semaphore_wait(barrier, len(greeted))

    sent = []

    def piece(origin, h, c, sem, other):
        return pltpu.make_async_remote_copy(
            src_ref=whole.at[origin, h, c],
            dst_ref=whole.at[origin, h, c],
            send_sem=sem,
            recv_sem=recv.at[origin, h, c],
            device_id=other,
            device_id_type=MESH,
        )

    def send(origin, h, sem, other):
        copy = piece(origin, h, core, sem, other)
        copy.start()
        sent.append(copy)

    def landed(origin, h, c):
        piece(origin, h, c, to_sibling.at[origin, h], sibling).wait_recv()

    send(place, side, to_ahead.at[place], ahead)
    send(place, side, to_behind.at[place], behind)
    for h in range(2):
        send(place, h, to_sibling.at[place, h], sibling)
    kv_copies = []
    for o in offsets:
        copy = pltpu.make_async_remote_copy(
            src_ref=picked.at[o + REACH],
            dst_ref=arrived.at[o + REACH],
            send_sem=kv_send.at[o + REACH],
            recv_sem=kv_recv.at[o + REACH],
            device_id=near(o),
            device_id_type=MESH,
        )
        copy.start()
        kv_copies.append(copy)
    own = pltpu.make_async_copy(picked.at[REACH], arrived.at[REACH], kv_own)
    own.start()

    tile = 32
    part = normed.shape[2]

    @pl.loop(0, hidden.shape[0] // tile)
    def _(i):
        rows = pl.ds(pl.multiple_of(i * tile, tile), tile)
        widened = hidden[rows, :].astype(jnp.float32)
        scale_inv = lax.rsqrt(jnp.mean(widened * widened, axis=-1, keepdims=True) + 1e-06)
        scaled = (widened * scale_inv * gain[...]).astype(jnp.bfloat16)
        for chip in range(chips):
            normed[chip, rows, :] = scaled[:, chip * part : (chip + 1) * part]

    columns = 256

    def multiply(origin, first):
        for h in range(2):
            landed(origin, h, 1 - core)

        @pl.loop(0, 2 * (width // columns))
        def _(i):
            h = lax.div(i, width // columns)
            t = lax.rem(i, width // columns)
            cols = pl.ds(pl.multiple_of(t * columns, columns), columns)
            block = whole[origin, h, :, :, cols].reshape(2 * depth, columns)
            product = jnp.dot(normed[origin], block, preferred_element_type=jnp.float32)
            if first:
                acc[h, :, cols] = product
            else:
                acc[h, :, cols] += product

    def origins(k):
        return [chip_of(spot - turn * k)] + ([chip_of(spot + turn * k)] if k < half else [])

    def from_ring(k):
        for origin, sem, other, last in zip(
            origins(k), (to_ahead, to_behind), (ahead, behind), (half, half - 1)
        ):
            landed(origin, side, core)
            if k < last:
                send(origin, side, sem.at[origin], other)
            send(origin, side, to_partner.at[origin], partner)
            send(origin, side, to_sibling.at[origin, side], sibling)

    def from_partner(k):
        for origin in origins(k):
            landed(origin, 1 - side, core)
            send(origin, 1 - side, to_sibling.at[origin, 1 - side], sibling)

    def multiply_step(k):
        for origin in origins(k):
            multiply(origin, False)

    multiply(place, True)
    for k in range(1, half + 4):
        if k <= half:
            from_ring(k)
        if 1 <= k - 2 <= half:
            from_partner(k - 2)
        if 1 <= k - 3 <= half:
            multiply_step(k - 3)

    for h in range(2):
        for t in range(width // columns):
            lane = h * width + t * columns
            query[:, lane : lane + columns] = (
                acc[h, :, t * columns : (t + 1) * columns] + bias[:, lane : lane + columns]
            ).astype(jnp.bfloat16)
    for copy in sent:
        copy.wait_send()
    for copy in kv_copies:
        copy.wait()
    own.wait()


def projected(hidden, norm_gain, q_weight, q_bias, picked):
    rows, features = hidden.shape
    depth, outputs = q_weight.shape
    chips = lax.axis_size("blk") // 2
    vmem = pl.BlockSpec(memory_space=pltpu.VMEM)
    anywhere = pl.BlockSpec(memory_space=pl.ANY)
    dma = pltpu.SemaphoreType.DMA
    span = 2 * REACH + 1
    return pl.pallas_call(
        functools.partial(project_kernel, chips, lax.axis_size("groups") == 2),
        out_shape=(
            jax.ShapeDtypeStruct((rows, outputs), jnp.bfloat16),
            jax.ShapeDtypeStruct(picked.shape, picked.dtype),
        ),
        in_specs=[vmem, vmem, vmem, vmem, anywhere],
        out_specs=(vmem, anywhere),
        scratch_shapes=[
            pltpu.VMEM((chips, 2, 2, depth, outputs // 2), jnp.bfloat16),
            pltpu.VMEM((chips, rows, features // chips), jnp.bfloat16),
            pltpu.VMEM((2, rows, outputs // 2), jnp.float32),
            dma((chips, 2, 2)),
            dma((chips,)),
            dma((chips,)),
            dma((chips, 2)),
            dma((chips,)),
            dma((span,)),
            dma((span,)),
            dma,
        ],
        compiler_params=pltpu.CompilerParams(
            collective_id=1, has_side_effects=True, vmem_limit_bytes=56 * 1024 * 1024
        ),
        cost_estimate=pl.CostEstimate(
            flops=2 * rows * features * outputs,
            bytes_accessed=2 * picked.size * 2 + rows * features * 2,
            transcendentals=0,
        ),
    )(hidden, norm_gain.reshape(1, -1), q_weight, q_bias.reshape(1, -1), picked)


def attend_kernel(slots, hole, fill, q_ref, first_ref, second_ref, out_ref):
    cand = pl.program_id(0)
    rows = q_ref.shape[0]
    factor = math.log2(math.e) / math.sqrt(HEAD_SIZE)
    live = fill[cand]
    start = hole[cand]
    column = lax.broadcasted_iota(jnp.int32, (rows, BLOCK_TOKENS), 1)
    masked = (column >= start) & (column < start + live)
    alive = lax.broadcasted_iota(jnp.int32, (rows, HEAD_SIZE), 0) < live
    over_keys = (((1,), (1,)), ((), ()))
    for head in range(QUERY_HEADS // KEY_HEADS):
        place = pl.ds(head * HEAD_SIZE, HEAD_SIZE)
        q = q_ref[:, place]
        near = lax.dot_general(q, first_ref[0, 0], over_keys, preferred_element_type=jnp.float32)
        far = lax.dot_general(q, second_ref[0, 0], over_keys, preferred_element_type=jnp.float32)
        near = jnp.where(masked, jnp.float32(-1e30), near)
        most = jnp.maximum(
            jnp.max(near, axis=-1, keepdims=True), jnp.max(far, axis=-1, keepdims=True)
        )
        near = jnp.exp2((near - most) * factor)
        far = jnp.exp2((far - most) * factor)
        total = jnp.sum(near, axis=-1, keepdims=True) + jnp.sum(far, axis=-1, keepdims=True)
        mixed = jnp.dot(
            near.astype(jnp.bfloat16), first_ref[0, 1], preferred_element_type=jnp.float32
        ) + jnp.dot(
            far.astype(jnp.bfloat16), second_ref[0, 1], preferred_element_type=jnp.float32
        )
        out_ref[:, place] = jnp.where(alive, mixed / total, 0.0).astype(jnp.bfloat16)


def attend(query, arrived, slots, need_ids, hole_pos, fill_len):
    cands = need_ids.shape[0]
    rows = query.shape[0] // cands
    width = QUERY_HEADS // KEY_HEADS * HEAD_SIZE
    hole = hole_pos - need_ids[:, 0] * BLOCK_TOKENS

    def sketch(entry):
        return pl.BlockSpec(
            (1, 2, BLOCK_TOKENS, HEAD_SIZE),
            lambda c, k, slots, hole, fill: (slots[c * BLOCKS_NEEDED + entry], 0, 0, k),
        )

    by_head = pl.BlockSpec((rows, width), lambda c, k, slots, hole, fill: (c, k))
    return pl.pallas_call(
        attend_kernel,
        grid_spec=pltpu.PrefetchScalarGridSpec(
            num_scalar_prefetch=3,
            grid=(cands, KEY_HEADS),
            in_specs=[by_head, sketch(0), sketch(1)],
            out_specs=by_head,
        ),
        out_shape=jax.ShapeDtypeStruct(query.shape, jnp.bfloat16),
        compiler_params=pltpu.CompilerParams(vmem_limit_bytes=40 * 1024 * 1024),
    )(slots.reshape(-1), hole, fill_len, query, arrived, arrived)


def shards(hidden, norm_gain, q_weight, q_bias, kv_store, block_home, need_ids, hole_pos, fill_len):
    device_count = lax.axis_size("blk")
    myself = lax.axis_index("blk")
    local_count = kv_store.shape[0]
    stored_at = block_home[exchanged(need_ids)]
    owned_here = stored_at // local_count == myself
    slots = jnp.sum(jnp.where(owned_here, stored_at % local_count, 0), axis=1)
    picked = picked_blocks(slots, kv_store)
    query, arrived = projected(hidden, norm_gain, q_weight, q_bias, picked)
    owners = block_home[need_ids] // local_count
    slot_of_entry = jnp.remainder(myself - owners + REACH, device_count)
    return attend(query, arrived, slot_of_entry, need_ids, hole_pos, fill_len)


def solution(mesh):
    placed = (
        P(("groups", "blk"), None),
        P(),
        P("blk", None),
        P(),
        P(("groups", "blk"), None, None, None),
        P("groups"),
        P(("groups", "blk"), None),
        P(("groups", "blk")),
        P(("groups", "blk")),
    )
    return jax.shard_map(
        shards, mesh=mesh, in_specs=placed, out_specs=P(("groups", "blk"), None), check_vma=False
    )
```

```python
import functools
import math

import jax
import jax.numpy as jnp
from jax import lax
from jax.experimental import pallas as pl
from jax.experimental.pallas import tpu as pltpu
from jax.sharding import PartitionSpec as P

HEAD_SIZE = 128
QUERY_HEADS = 20
KEY_HEADS = 4
BLOCK_TOKENS = 512
BLOCKS_NEEDED = 2
REACH = 2
MESH = pl.DeviceIdType.MESH
CHUNKS = 2
KV_STEP = 4


def exchange_kernel(ids_ref, out_ref, send_sem, recv_sem):
    count = lax.axis_size("blk")
    me = lax.axis_index("blk")
    barrier = pltpu.get_barrier_semaphore()
    offsets = [o for o in range(-REACH, REACH + 1) if o]
    for o in offsets:
        pl.semaphore_signal(
            barrier, inc=1, device_id={"blk": lax.rem(me + o + count, count)}, device_id_type=MESH
        )
    pl.semaphore_wait(barrier, len(offsets))
    copies = []
    for o in offsets:
        copy = pltpu.make_async_remote_copy(
            src_ref=ids_ref,
            dst_ref=out_ref.at[o + REACH],
            send_sem=send_sem.at[o + REACH],
            recv_sem=recv_sem.at[o + REACH],
            device_id={"blk": lax.rem(me - o + count, count)},
            device_id_type=MESH,
        )
        copy.start()
        copies.append(copy)
    out_ref[REACH] = ids_ref[...]
    for copy in copies:
        copy.wait()


def exchanged(need_ids):
    cands, needed = need_ids.shape
    padded = jnp.pad(need_ids, ((0, 8 - cands), (0, 128 - needed)))
    span = 2 * REACH + 1
    out = pl.pallas_call(
        exchange_kernel,
        out_shape=jax.ShapeDtypeStruct((span, 8, 128), jnp.int32),
        in_specs=[pl.BlockSpec(memory_space=pltpu.VMEM)],
        out_specs=pl.BlockSpec(memory_space=pltpu.VMEM),
        scratch_shapes=[pltpu.SemaphoreType.DMA((span,)), pltpu.SemaphoreType.DMA((span,))],
        compiler_params=pltpu.CompilerParams(collective_id=0, has_side_effects=True),
    )(padded)
    return out[:, :cands, :needed].reshape(span, cands * needed)


def pick_kernel(slots, in_ref, out_ref):
    out_ref[...] = in_ref[...]


def picked_blocks(slots, kv_store):
    block = (1,) + kv_store.shape[1:]
    return pl.pallas_call(
        pick_kernel,
        grid_spec=pltpu.PrefetchScalarGridSpec(
            num_scalar_prefetch=1,
            grid=slots.shape,
            in_specs=[pl.BlockSpec(block, lambda i, slots: (slots[i], 0, 0, 0))],
            out_specs=pl.BlockSpec(block, lambda i, slots: (i, 0, 0, 0)),
        ),
        out_shape=jax.ShapeDtypeStruct(slots.shape + kv_store.shape[1:], kv_store.dtype),
        compiler_params=pltpu.CompilerParams(vmem_limit_bytes=58 * 1024 * 1024),
    )(slots, kv_store)


def project_kernel(
    chips, snake, hidden_far, gain, weight, bias, picked, query, arrived,
    whole, normed, acc, recv, to_ahead, to_behind, to_sibling, to_partner, kv_send, kv_recv, kv_own,
    hidden, hidden_sem,
):
    group, me = lax.axis_index("groups"), lax.axis_index("blk")
    count = 2 * chips
    half = chips // 2
    place, core, side = lax.div(me, 2), lax.rem(me, 2), lax.rem(group, 2)
    depth, width = weight.shape[0], weight.shape[1] // (2 * CHUNKS)

    def ring_of(chip):
        if not snake:
            return chip
        z, y = lax.div(chip, 2), lax.rem(chip, 2)
        return z + y * (chips - 1 - 2 * z)

    def chip_of(spot):
        spot = lax.rem(spot + chips, chips)
        if not snake:
            return spot
        y = lax.div(spot, half)
        return (spot + y * (chips - 1 - 2 * spot)) * 2 + y

    spot = ring_of(place)
    turn = 1 - 2 * core
    ahead = {"blk": chip_of(spot + turn) * 2 + core}
    behind = {"blk": chip_of(spot - turn) * 2 + core}
    sibling = {"blk": me + turn}
    partner = {"groups": group + 1 - 2 * side}
    offsets = [o for o in (1, -1, 2, -2)]

    def near(o):
        return {"blk": lax.rem(me + o + count, count)}

    greeted = [ahead, behind, sibling, partner] + [near(o) for o in offsets]
    fetch = pltpu.make_async_copy(hidden_far, hidden, hidden_sem)
    fetch.start()
    barrier = pltpu.get_barrier_semaphore()
    for other in greeted:
        pl.semaphore_signal(barrier, inc=1, device_id=other, device_id_type=MESH)
    for h in range(2 * CHUNKS):
        whole[place, h, core] = weight[:, h * width : (h + 1) * width]
    pl.semaphore_wait(barrier, len(greeted))

    sent = []

    def piece(origin, h, c, sem, other):
        return pltpu.make_async_remote_copy(
            src_ref=whole.at[origin, h, c],
            dst_ref=whole.at[origin, h, c],
            send_sem=sem,
            recv_sem=recv.at[origin, h, c],
            device_id=other,
            device_id_type=MESH,
        )

    def send(origin, h, sem, other):
        copy = piece(origin, h, core, sem, other)
        copy.start()
        sent.append(copy)

    def landed(origin, h, c):
        piece(origin, h, c, to_sibling.at[origin, h], sibling).wait_recv()

    for j in range(CHUNKS):
        send(place, side * CHUNKS + j, to_ahead.at[place, j], ahead)
        send(place, side * CHUNKS + j, to_behind.at[place, j], behind)
    for h in range(2 * CHUNKS):
        send(place, h, to_sibling.at[place, h], sibling)
    kv_copies = []
    for o in offsets:
        copy = pltpu.make_async_remote_copy(
            src_ref=picked.at[o + REACH],
            dst_ref=arrived.at[o + REACH],
            send_sem=kv_send.at[o + REACH],
            recv_sem=kv_recv.at[o + REACH],
            device_id=near(o),
            device_id_type=MESH,
        )
        kv_copies.append(copy)
    own = pltpu.make_async_copy(picked.at[REACH], arrived.at[REACH], kv_own)
    own.start()

    fetch.wait()
    tile = 32
    part = normed.shape[2]

    @pl.loop(0, hidden.shape[0] // tile)
    def _(i):
        rows = pl.ds(pl.multiple_of(i * tile, tile), tile)
        widened = hidden[rows, :].astype(jnp.float32)
        scale_inv = lax.rsqrt(jnp.mean(widened * widened, axis=-1, keepdims=True) + 1e-06)
        scaled = (widened * scale_inv * gain[...]).astype(jnp.bfloat16)
        for chip in range(chips):
            normed[chip, rows, :] = scaled[:, chip * part : (chip + 1) * part]

    def multiply(origin, first):
        for h in range(2 * CHUNKS):
            landed(origin, h, 1 - core)

        @pl.loop(0, 2 * CHUNKS)
        def _(h):
            block = whole[origin, h].reshape(2 * depth, width)
            product = jnp.dot(normed[origin], block, preferred_element_type=jnp.float32)
            if first:
                acc[h] = product
            else:
                acc[h] += product

    def origins(k):
        return [chip_of(spot - turn * k)] + ([chip_of(spot + turn * k)] if k < half else [])

    def from_ring(k):
        for j in range(CHUNKS):
            h = side * CHUNKS + j
            for origin, sem, other, last in zip(
                origins(k), (to_ahead, to_behind), (ahead, behind), (half, half - 1)
            ):
                landed(origin, h, core)
                if k < last:
                    send(origin, h, sem.at[origin, j], other)
                send(origin, h, to_partner.at[origin, j], partner)
                send(origin, h, to_sibling.at[origin, h], sibling)

    def from_partner(k):
        for j in range(CHUNKS):
            h = (1 - side) * CHUNKS + j
            for origin in origins(k):
                landed(origin, h, core)
                send(origin, h, to_sibling.at[origin, h], sibling)

    def multiply_step(k):
        for origin in origins(k):
            multiply(origin, False)

    multiply(place, True)
    for k in range(1, half + 4):
        if k == KV_STEP:
            for copy in kv_copies:
                copy.start()
        if k <= half:
            from_ring(k)
        if 1 <= k - 2 <= half:
            from_partner(k - 2)
        if 1 <= k - 3 <= half:
            multiply_step(k - 3)

    for h in range(2 * CHUNKS):
        lanes = slice(h * width, (h + 1) * width)
        query[:, lanes] = (acc[h] + bias[:, lanes]).astype(jnp.bfloat16)
    for copy in sent:
        copy.wait_send()
    for copy in kv_copies:
        copy.wait()
    own.wait()


def projected(hidden, norm_gain, q_weight, q_bias, picked):
    rows, features = hidden.shape
    depth, outputs = q_weight.shape
    chips = lax.axis_size("blk") // 2
    vmem = pl.BlockSpec(memory_space=pltpu.VMEM)
    anywhere = pl.BlockSpec(memory_space=pl.ANY)
    dma = pltpu.SemaphoreType.DMA
    span = 2 * REACH + 1
    return pl.pallas_call(
        functools.partial(project_kernel, chips, lax.axis_size("groups") == 2),
        out_shape=(
            jax.ShapeDtypeStruct((rows, outputs), jnp.bfloat16),
            jax.ShapeDtypeStruct(picked.shape, picked.dtype),
        ),
        in_specs=[anywhere, vmem, vmem, vmem, anywhere],
        out_specs=(vmem, anywhere),
        scratch_shapes=[
            pltpu.VMEM((chips, 2 * CHUNKS, 2, depth, outputs // (2 * CHUNKS)), jnp.bfloat16),
            pltpu.VMEM((chips, rows, features // chips), jnp.bfloat16),
            pltpu.VMEM((2 * CHUNKS, rows, outputs // (2 * CHUNKS)), jnp.float32),
            dma((chips, 2 * CHUNKS, 2)),
            dma((chips, CHUNKS)),
            dma((chips, CHUNKS)),
            dma((chips, 2 * CHUNKS)),
            dma((chips, CHUNKS)),
            dma((span,)),
            dma((span,)),
            dma,
            pltpu.VMEM((rows, features), jnp.bfloat16),
            dma,
        ],
        compiler_params=pltpu.CompilerParams(
            collective_id=1, has_side_effects=True, vmem_limit_bytes=58 * 1024 * 1024
        ),
        cost_estimate=pl.CostEstimate(
            flops=2 * rows * features * outputs,
            bytes_accessed=2 * picked.size * 2 + rows * features * 2,
            transcendentals=0,
        ),
    )(hidden, norm_gain.reshape(1, -1), q_weight, q_bias.reshape(1, -1), picked)


def attend_kernel(slots, hole, fill, q_ref, first_ref, second_ref, out_ref):
    cand = pl.program_id(0)
    rows = q_ref.shape[0]
    factor = math.log2(math.e) / math.sqrt(HEAD_SIZE)
    live = fill[cand]
    start = hole[cand]
    column = lax.broadcasted_iota(jnp.int32, (rows, BLOCK_TOKENS), 1)
    masked = (column >= start) & (column < start + live)
    alive = lax.broadcasted_iota(jnp.int32, (rows, HEAD_SIZE), 0) < live
    over_keys = (((1,), (1,)), ((), ()))
    for head in range(QUERY_HEADS // KEY_HEADS):
        place = pl.ds(head * HEAD_SIZE, HEAD_SIZE)
        q = q_ref[:, place]
        near = lax.dot_general(q, first_ref[0, 0], over_keys, preferred_element_type=jnp.float32)
        far = lax.dot_general(q, second_ref[0, 0], over_keys, preferred_element_type=jnp.float32)
        near = jnp.where(masked, jnp.float32(-1e30), near)
        most = jnp.maximum(
            jnp.max(near, axis=-1, keepdims=True), jnp.max(far, axis=-1, keepdims=True)
        )
        near = jnp.exp2((near - most) * factor)
        far = jnp.exp2((far - most) * factor)
        total = jnp.sum(near, axis=-1, keepdims=True) + jnp.sum(far, axis=-1, keepdims=True)
        mixed = jnp.dot(
            near.astype(jnp.bfloat16), first_ref[0, 1], preferred_element_type=jnp.float32
        ) + jnp.dot(
            far.astype(jnp.bfloat16), second_ref[0, 1], preferred_element_type=jnp.float32
        )
        out_ref[:, place] = jnp.where(alive, mixed / total, 0.0).astype(jnp.bfloat16)


def attend(query, arrived, slots, need_ids, hole_pos, fill_len):
    cands = need_ids.shape[0]
    rows = query.shape[0] // cands
    width = QUERY_HEADS // KEY_HEADS * HEAD_SIZE
    hole = hole_pos - need_ids[:, 0] * BLOCK_TOKENS

    def sketch(entry):
        return pl.BlockSpec(
            (1, 2, BLOCK_TOKENS, HEAD_SIZE),
            lambda c, k, slots, hole, fill: (slots[c * BLOCKS_NEEDED + entry], 0, 0, k),
        )

    by_head = pl.BlockSpec((rows, width), lambda c, k, slots, hole, fill: (c, k))
    return pl.pallas_call(
        attend_kernel,
        grid_spec=pltpu.PrefetchScalarGridSpec(
            num_scalar_prefetch=3,
            grid=(cands, KEY_HEADS),
            in_specs=[by_head, sketch(0), sketch(1)],
            out_specs=by_head,
        ),
        out_shape=jax.ShapeDtypeStruct(query.shape, jnp.bfloat16),
        compiler_params=pltpu.CompilerParams(vmem_limit_bytes=58 * 1024 * 1024),
    )(slots.reshape(-1), hole, fill_len, query, arrived, arrived)


def shards(hidden, norm_gain, q_weight, q_bias, kv_store, block_home, need_ids, hole_pos, fill_len):
    device_count = lax.axis_size("blk")
    myself = lax.axis_index("blk")
    local_count = kv_store.shape[0]
    stored_at = block_home[exchanged(need_ids)]
    owned_here = stored_at // local_count == myself
    slots = jnp.sum(jnp.where(owned_here, stored_at % local_count, 0), axis=1)
    picked = picked_blocks(slots, kv_store)
    query, arrived = projected(hidden, norm_gain, q_weight, q_bias, picked)
    owners = block_home[need_ids] // local_count
    slot_of_entry = jnp.remainder(myself - owners + REACH, device_count)
    return attend(query, arrived, slot_of_entry, need_ids, hole_pos, fill_len)


def solution(mesh):
    placed = (
        P(("groups", "blk"), None),
        P(),
        P("blk", None),
        P(),
        P(("groups", "blk"), None, None, None),
        P("groups"),
        P(("groups", "blk"), None),
        P(("groups", "blk")),
        P(("groups", "blk")),
    )
    return jax.shard_map(
        shards, mesh=mesh, in_specs=placed, out_specs=P(("groups", "blk"), None), check_vma=False
    )
```

```python
import functools
import math

import jax
import jax.numpy as jnp
from jax import lax
from jax.experimental import pallas as pl
from jax.experimental.pallas import tpu as pltpu
from jax.sharding import PartitionSpec as P

HEAD_SIZE = 128
QUERY_HEADS = 20
KEY_HEADS = 4
BLOCK_TOKENS = 512
BLOCKS_NEEDED = 2
REACH = 2
MESH = pl.DeviceIdType.MESH
CHUNKS = 2
KV_STEP = 3


def exchange_kernel(ids_ref, out_ref, send_sem, recv_sem):
    count = lax.axis_size("blk")
    me = lax.axis_index("blk")
    barrier = pltpu.get_barrier_semaphore()
    offsets = [o for o in range(-REACH, REACH + 1) if o]
    for o in offsets:
        pl.semaphore_signal(
            barrier, inc=1, device_id={"blk": lax.rem(me + o + count, count)}, device_id_type=MESH
        )
    pl.semaphore_wait(barrier, len(offsets))
    copies = []
    for o in offsets:
        copy = pltpu.make_async_remote_copy(
            src_ref=ids_ref,
            dst_ref=out_ref.at[o + REACH],
            send_sem=send_sem.at[o + REACH],
            recv_sem=recv_sem.at[o + REACH],
            device_id={"blk": lax.rem(me - o + count, count)},
            device_id_type=MESH,
        )
        copy.start()
        copies.append(copy)
    out_ref[REACH] = ids_ref[...]
    for copy in copies:
        copy.wait()


def exchanged(need_ids):
    cands, needed = need_ids.shape
    padded = jnp.pad(need_ids, ((0, 8 - cands), (0, 128 - needed)))
    span = 2 * REACH + 1
    out = pl.pallas_call(
        exchange_kernel,
        out_shape=jax.ShapeDtypeStruct((span, 8, 128), jnp.int32),
        in_specs=[pl.BlockSpec(memory_space=pltpu.VMEM)],
        out_specs=pl.BlockSpec(memory_space=pltpu.VMEM),
        scratch_shapes=[pltpu.SemaphoreType.DMA((span,)), pltpu.SemaphoreType.DMA((span,))],
        compiler_params=pltpu.CompilerParams(collective_id=0, has_side_effects=True),
    )(padded)
    return out[:, :cands, :needed].reshape(span, cands * needed)


def pick_kernel(slots, in_ref, out_ref):
    out_ref[...] = in_ref[...]


def picked_blocks(slots, kv_store):
    block = (1,) + kv_store.shape[1:]
    return pl.pallas_call(
        pick_kernel,
        grid_spec=pltpu.PrefetchScalarGridSpec(
            num_scalar_prefetch=1,
            grid=slots.shape,
            in_specs=[pl.BlockSpec(block, lambda i, slots: (slots[i], 0, 0, 0))],
            out_specs=pl.BlockSpec(block, lambda i, slots: (i, 0, 0, 0)),
        ),
        out_shape=jax.ShapeDtypeStruct(slots.shape + kv_store.shape[1:], kv_store.dtype),
        compiler_params=pltpu.CompilerParams(vmem_limit_bytes=16 * 1024 * 1024),
    )(slots, kv_store)


def project_kernel(
    chips, snake, hidden_far, gain, weight, bias, picked, query, arrived,
    whole, normed, acc, recv, to_ahead, to_behind, to_sibling, to_partner, kv_send, kv_recv, kv_own,
    hidden, hidden_sem,
):
    group, me = lax.axis_index("groups"), lax.axis_index("blk")
    count = 2 * chips
    half = chips // 2
    place, core, side = lax.div(me, 2), lax.rem(me, 2), lax.rem(group, 2)
    depth, width = weight.shape[0], weight.shape[1] // (2 * CHUNKS)

    def ring_of(chip):
        if not snake:
            return chip
        z, y = lax.div(chip, 2), lax.rem(chip, 2)
        return z + y * (chips - 1 - 2 * z)

    def chip_of(spot):
        spot = lax.rem(spot + chips, chips)
        if not snake:
            return spot
        y = lax.div(spot, half)
        return (spot + y * (chips - 1 - 2 * spot)) * 2 + y

    spot = ring_of(place)
    turn = 1 - 2 * core
    ahead = {"blk": chip_of(spot + turn) * 2 + core}
    behind = {"blk": chip_of(spot - turn) * 2 + core}
    sibling = {"blk": me + turn}
    partner = {"groups": group + 1 - 2 * side}
    offsets = [o for o in (2, -2, 1, -1)]

    def near(o):
        return {"blk": lax.rem(me + o + count, count)}

    greeted = [ahead, behind, sibling, partner] + [near(o) for o in offsets]
    fetch = pltpu.make_async_copy(hidden_far, hidden, hidden_sem)
    fetch.start()
    barrier = pltpu.get_barrier_semaphore()
    for other in greeted:
        pl.semaphore_signal(barrier, inc=1, device_id=other, device_id_type=MESH)
    for h in range(2 * CHUNKS):
        whole[place, h, core] = weight[:, h * width : (h + 1) * width]
    pl.semaphore_wait(barrier, len(greeted))

    sent = []

    def piece(origin, h, c, sem, other):
        return pltpu.make_async_remote_copy(
            src_ref=whole.at[origin, h, c],
            dst_ref=whole.at[origin, h, c],
            send_sem=sem,
            recv_sem=recv.at[origin, h, c],
            device_id=other,
            device_id_type=MESH,
        )

    def send(origin, h, sem, other):
        copy = piece(origin, h, core, sem, other)
        copy.start()
        sent.append(copy)

    def landed(origin, h, c):
        piece(origin, h, c, to_sibling.at[origin, h], sibling).wait_recv()

    for j in range(CHUNKS):
        send(place, side * CHUNKS + j, to_ahead.at[place, j], ahead)
        send(place, side * CHUNKS + j, to_behind.at[place, j], behind)
    for h in range(2 * CHUNKS):
        send(place, h, to_sibling.at[place, h], sibling)
    kv_copies = []
    for o in offsets:
        copy = pltpu.make_async_remote_copy(
            src_ref=picked.at[o + REACH],
            dst_ref=arrived.at[o + REACH],
            send_sem=kv_send.at[o + REACH],
            recv_sem=kv_recv.at[o + REACH],
            device_id=near(o),
            device_id_type=MESH,
        )
        kv_copies.append(copy)
    own = pltpu.make_async_copy(picked.at[REACH], arrived.at[REACH], kv_own)
    own.start()

    fetch.wait()
    tile = 32
    part = normed.shape[2]

    @pl.loop(0, hidden.shape[0] // tile)
    def _(i):
        rows = pl.ds(pl.multiple_of(i * tile, tile), tile)
        widened = hidden[rows, :].astype(jnp.float32)
        scale_inv = lax.rsqrt(jnp.mean(widened * widened, axis=-1, keepdims=True) + 1e-06)
        scaled = (widened * scale_inv * gain[...]).astype(jnp.bfloat16)
        for chip in range(chips):
            normed[chip, rows, :] = scaled[:, chip * part : (chip + 1) * part]

    def multiply(origin, first):
        for h in range(2 * CHUNKS):
            landed(origin, h, 1 - core)

        @pl.loop(0, 2 * CHUNKS)
        def _(h):
            block = whole[origin, h].reshape(2 * depth, width)
            product = jnp.dot(normed[origin], block, preferred_element_type=jnp.float32)
            if first:
                acc[h] = product
            else:
                acc[h] += product

    def origins(k):
        return [chip_of(spot - turn * k)] + ([chip_of(spot + turn * k)] if k < half else [])

    def from_ring(k):
        for j in range(CHUNKS):
            h = side * CHUNKS + j
            for origin, sem, other, last in zip(
                origins(k), (to_ahead, to_behind), (ahead, behind), (half, half - 1)
            ):
                landed(origin, h, core)
                if k < last:
                    send(origin, h, sem.at[origin, j], other)
                send(origin, h, to_partner.at[origin, j], partner)
                send(origin, h, to_sibling.at[origin, h], sibling)

    def from_partner(k):
        for j in range(CHUNKS):
            h = (1 - side) * CHUNKS + j
            for origin in origins(k):
                landed(origin, h, core)
                send(origin, h, to_sibling.at[origin, h], sibling)

    def multiply_step(k):
        for origin in origins(k):
            multiply(origin, False)

    multiply(place, True)
    for k in range(1, half + 4):
        if k <= half:
            from_ring(k)
        if k == KV_STEP:
            for copy in kv_copies:
                copy.start()
        if 1 <= k - 2 <= half:
            from_partner(k - 2)
        if 1 <= k - 3 <= half:
            multiply_step(k - 3)

    for h in range(2 * CHUNKS):
        lanes = slice(h * width, (h + 1) * width)
        query[:, lanes] = (acc[h] + bias[:, lanes]).astype(jnp.bfloat16)
    for copy in sent:
        copy.wait_send()
    for copy in kv_copies:
        copy.wait()
    own.wait()


def projected(hidden, norm_gain, q_weight, q_bias, picked):
    rows, features = hidden.shape
    depth, outputs = q_weight.shape
    chips = lax.axis_size("blk") // 2
    vmem = pl.BlockSpec(memory_space=pltpu.VMEM)
    anywhere = pl.BlockSpec(memory_space=pl.ANY)
    dma = pltpu.SemaphoreType.DMA
    span = 2 * REACH + 1
    return pl.pallas_call(
        functools.partial(project_kernel, chips, lax.axis_size("groups") == 2),
        out_shape=(
            jax.ShapeDtypeStruct((rows, outputs), jnp.bfloat16),
            jax.ShapeDtypeStruct(picked.shape, picked.dtype),
        ),
        in_specs=[anywhere, vmem, vmem, vmem, anywhere],
        out_specs=(vmem, anywhere),
        scratch_shapes=[
            pltpu.VMEM((chips, 2 * CHUNKS, 2, depth, outputs // (2 * CHUNKS)), jnp.bfloat16),
            pltpu.VMEM((chips, rows, features // chips), jnp.bfloat16),
            pltpu.VMEM((2 * CHUNKS, rows, outputs // (2 * CHUNKS)), jnp.float32),
            dma((chips, 2 * CHUNKS, 2)),
            dma((chips, CHUNKS)),
            dma((chips, CHUNKS)),
            dma((chips, 2 * CHUNKS)),
            dma((chips, CHUNKS)),
            dma((span,)),
            dma((span,)),
            dma,
            pltpu.VMEM((rows, features), jnp.bfloat16),
            dma,
        ],
        compiler_params=pltpu.CompilerParams(
            collective_id=1, has_side_effects=True, vmem_limit_bytes=58 * 1024 * 1024
        ),
        cost_estimate=pl.CostEstimate(
            flops=2 * rows * features * outputs,
            bytes_accessed=2 * picked.size * 2 + rows * features * 2,
            transcendentals=0,
        ),
    )(hidden, norm_gain.reshape(1, -1), q_weight, q_bias.reshape(1, -1), picked)


def attend_kernel(slots, hole, fill, q_ref, first_ref, second_ref, out_ref):
    cand = pl.program_id(0)
    rows = q_ref.shape[0]
    factor = math.log2(math.e) / math.sqrt(HEAD_SIZE)
    live = fill[cand]
    start = hole[cand]
    column = lax.broadcasted_iota(jnp.int32, (rows, BLOCK_TOKENS), 1)
    masked = (column >= start) & (column < start + live)
    alive = lax.broadcasted_iota(jnp.int32, (rows, HEAD_SIZE), 0) < live
    over_keys = (((1,), (1,)), ((), ()))
    for head in range(QUERY_HEADS // KEY_HEADS):
        place = pl.ds(head * HEAD_SIZE, HEAD_SIZE)
        q = q_ref[:, place]
        near = lax.dot_general(q, first_ref[0, 0], over_keys, preferred_element_type=jnp.float32)
        far = lax.dot_general(q, second_ref[0, 0], over_keys, preferred_element_type=jnp.float32)
        near = jnp.where(masked, jnp.float32(-1e30), near)
        most = jnp.maximum(
            jnp.max(near, axis=-1, keepdims=True), jnp.max(far, axis=-1, keepdims=True)
        )
        near = jnp.exp2((near - most) * factor)
        far = jnp.exp2((far - most) * factor)
        total = jnp.sum(near, axis=-1, keepdims=True) + jnp.sum(far, axis=-1, keepdims=True)
        mixed = jnp.dot(
            near.astype(jnp.bfloat16), first_ref[0, 1], preferred_element_type=jnp.float32
        ) + jnp.dot(
            far.astype(jnp.bfloat16), second_ref[0, 1], preferred_element_type=jnp.float32
        )
        out_ref[:, place] = jnp.where(alive, mixed / total, 0.0).astype(jnp.bfloat16)


def attend(query, arrived, slots, need_ids, hole_pos, fill_len):
    cands = need_ids.shape[0]
    rows = query.shape[0] // cands
    width = QUERY_HEADS // KEY_HEADS * HEAD_SIZE
    hole = hole_pos - need_ids[:, 0] * BLOCK_TOKENS

    def sketch(entry):
        return pl.BlockSpec(
            (1, 2, BLOCK_TOKENS, HEAD_SIZE),
            lambda c, k, slots, hole, fill: (slots[c * BLOCKS_NEEDED + entry], 0, 0, k),
        )

    by_head = pl.BlockSpec((rows, width), lambda c, k, slots, hole, fill: (c, k))
    return pl.pallas_call(
        attend_kernel,
        grid_spec=pltpu.PrefetchScalarGridSpec(
            num_scalar_prefetch=3,
            grid=(cands, KEY_HEADS),
            in_specs=[by_head, sketch(0), sketch(1)],
            out_specs=by_head,
        ),
        out_shape=jax.ShapeDtypeStruct(query.shape, jnp.bfloat16),
        compiler_params=pltpu.CompilerParams(vmem_limit_bytes=58 * 1024 * 1024),
    )(slots.reshape(-1), hole, fill_len, query, arrived, arrived)


def shards(hidden, norm_gain, q_weight, q_bias, kv_store, block_home, need_ids, hole_pos, fill_len):
    device_count = lax.axis_size("blk")
    myself = lax.axis_index("blk")
    local_count = kv_store.shape[0]
    stored_at = block_home[exchanged(need_ids)]
    owned_here = stored_at // local_count == myself
    slots = jnp.sum(jnp.where(owned_here, stored_at % local_count, 0), axis=1)
    picked = picked_blocks(slots, kv_store)
    query, arrived = projected(hidden, norm_gain, q_weight, q_bias, picked)
    owners = block_home[need_ids] // local_count
    slot_of_entry = jnp.remainder(myself - owners + REACH, device_count)
    return attend(query, arrived, slot_of_entry, need_ids, hole_pos, fill_len)


def solution(mesh):
    placed = (
        P(("groups", "blk"), None),
        P(),
        P("blk", None),
        P(),
        P(("groups", "blk"), None, None, None),
        P("groups"),
        P(("groups", "blk"), None),
        P(("groups", "blk")),
        P(("groups", "blk")),
    )
    return jax.shard_map(
        shards, mesh=mesh, in_specs=placed, out_specs=P(("groups", "blk"), None), check_vma=False
    )
```
